512 devices in a mesh: chain: 8 (over y, core), block: 64 (over z, x).
Axes of the slice: x: 4, y: 4, z: 16, core: 2. Of those that a mesh axis runs over, the one named last changes fastest.
Arguments:
- wave: float32 [8, 32768, 512], P('chain', 'block'), may hold values from -6 to 6
- diagonal: bfloat16 [8, 32768, 512], P('chain', 'block'), may hold values from 0.5 to 4
- left_env: bfloat16 [8, 128, 512, 512], P('chain', 'block'), may hold values from -0.125 to 0.125
- right_env: bfloat16 [8, 128, 512, 512], P('chain', 'block'), may hold values from -0.25 to 0.25
- pair_hop: int32 [128], P('block'), may hold values from 0 to 2
Outputs:
- wave_out: float32 [8, 32768, 512], P('chain', 'block')
- energies: float32 [8, 3], P('chain')
The draws below stay inside these ranges and needn't reach their ends.
All inputs are finite; a program needn't handle non-finite values.
Results may differ from the reference program's by a relative error of at most 0.003.
Values may be sent and summed in bfloat16 or wider, within the bound.
A program may use at most 64 MiB of HBM per device.

```python
import math
import jax
import jax.numpy as jnp
from jax import lax

BS = 512
PAIR_DEV = 2
ITERS = 3
NBLK = 64
NPAIR = 128
SEGS = 8


def touch_ends(drawn, stream_key, smallest, largest):
    place = [jax.random.randint(jax.random.fold_in(stream_key, axis), (), 0, length) for axis, length in enumerate(drawn.shape)]
    main_axis = drawn.shape.index(max(drawn.shape))
    beside = place[:main_axis] + [(place[main_axis] + 1) % drawn.shape[main_axis]] + place[main_axis + 1:]
    return drawn.at[tuple(place)].set(smallest).at[tuple(beside)].set(largest)


def block_levels(stream_key, shape, split, low, high):
    gain = 1.0
    for axis_at, parts in split:
        heights = jax.random.uniform(jax.random.fold_in(jax.random.fold_in(stream_key, 6), axis_at), (parts,), jnp.float32, low / len(split), high / len(split))
        gain = gain * jnp.repeat(jnp.exp(heights), shape[axis_at] // parts).reshape((-1,) + (1,) * (len(shape) - 1 - axis_at))
    return gain


def bell_draw(stream_key, extent, width, most, shards=(), kind=jnp.bfloat16):
    array = width * jax.random.normal(stream_key, extent, jnp.float32)
    if shards:
        array = array * block_levels(stream_key, extent, shards, -0.22, 0.18)
    return jnp.clip(array, -most, most).astype(kind)


def setup_inputs(seed: int = 0) -> dict:
    key_list = jax.random.split(jax.random.key(seed), 6)
    return {
        "wave": bell_draw(key_list[0], (SEGS, NBLK * BS, BS), 1.0, 6.0, ((0, 8), (1, 64)), jnp.float32),
        "diagonal": jnp.clip(jnp.exp(math.log(4.0) - 2.0794415 * jax.random.uniform(key_list[1], (SEGS, NBLK * BS, BS), jnp.float32) ** block_levels(key_list[1], (SEGS, NBLK * BS, BS), ((0, 8), (1, 64)), -0.2, 0.2)), 0.5, 4.0).astype(jnp.bfloat16),
        "left_env": bell_draw(key_list[2], (SEGS, NPAIR, BS, BS), (4 * BS) ** -0.5, 0.125, ((0, 8), (1, 64))),
        "right_env": bell_draw(key_list[3], (SEGS, NPAIR, BS, BS), BS ** -0.5, 0.25, ((0, 8), (1, 64))),
        "pair_hop": touch_ends(jax.random.randint(key_list[4], (NPAIR,), 0, 3), jax.random.fold_in(key_list[4], 1), 0, 2).astype(jnp.int32),
    }


HIGHEST = lax.Precision.HIGHEST
STEP_RATE = 0.3


def apply_terms(current, lefts, rights, pair_hop):
    blocks = current.reshape(NBLK, BS, BS).astype(jnp.bfloat16)
    empty = jnp.zeros((1, BS, BS), jnp.bfloat16)
    padded = jnp.concatenate([empty, blocks, empty], axis=0)
    out_block = jnp.arange(NPAIR, dtype=jnp.int32) // PAIR_DEV
    source = (out_block + pair_hop).astype(jnp.int32)
    inputs = padded[source]
    first = jnp.einsum('pab,pbr->par', lefts.astype(jnp.float32), inputs.astype(jnp.float32), precision=HIGHEST).astype(jnp.bfloat16)
    terms = jnp.einsum('par,pqr->paq', first.astype(jnp.float32), rights.astype(jnp.float32), precision=HIGHEST)
    return jnp.sum(terms.reshape(NBLK, PAIR_DEV, BS, BS), axis=1).reshape(NBLK * BS, BS)


def reference(wave, diagonal, left_env, right_env, pair_hop):
    handed = jnp.roll(left_env, 1, axis=0)
    results = []
    all_energies = []
    for segment in range(SEGS):
        current = wave[segment]
        diag_part = diagonal[segment].astype(jnp.float32)
        energies = []
        for iteration in range(ITERS):
            image = apply_terms(current, handed[segment], right_env[segment], pair_hop) + diag_part * current
            energy = jnp.sum(current * image) / jnp.sum(current * current)
            current = current - STEP_RATE * (image - energy * current)
            energies.append(energy)
        results.append(current)
        all_energies.append(jnp.stack(energies))
    return jnp.stack(results), jnp.stack(all_energies)
```

```python
import functools

import jax
import jax.numpy as jnp
from jax import lax
from jax.experimental import pallas as pl
from jax.experimental.pallas import tpu as pltpu
from jax.sharding import PartitionSpec as P

MESH = pl.DeviceIdType.MESH
BS = 512
ITERS = 3
RATE = 0.3
FIRST_SHIFT = 2.0
NCH = 4
CW = BS // NCH
XG = 4
F32 = jnp.float32
BF16 = jnp.bfloat16


def dot(a, b):
    return jnp.dot(a, b, preferred_element_type=F32)


def fold(values):
    return jnp.sum(values.reshape(BS // 8, 8, CW), axis=0)


def kernel(segs, nblk, *refs):
    (hop_hbm, wave_hbm, diag_hbm, left_hbm, right_hbm, out_hbm, en_ref) = refs[:7]
    refs = refs[7:]
    bufs = refs[: ITERS * NCH]
    refs = refs[ITERS * NCH:]
    (hop_s, x_v, diag_v, right_v, left_v, rt_v, d_v, dprev_v, c_v, b_v, im_v, out_v,
     xpart, zpart, in_sem, out_sem, l_send, l_recv, x_send, x_recv, s1_send, s1_recv, s2_send, s2_recv) = refs

    zg = nblk // XG
    c = lax.axis_index("chain")
    j = lax.axis_index("block")
    zi, xi = j // XG, j % XG
    up, down = (j + 1) % nblk, (j + nblk - 1) % nblk
    after, before = (c + 1) % segs, (c + segs - 1) % segs
    x_others = [zi * XG + (xi + d) % XG for d in range(1, XG)]
    x_slots = [(xi + d) % XG for d in range(1, XG)]
    z_others = [((zi + d) % zg) * XG + xi for d in range(1, zg)]
    z_slots = [(zi + d) % zg for d in range(1, zg)]

    barrier = pltpu.get_barrier_semaphore()
    partners = [{"block": t} for t in [up, down] + x_others + z_others] + [{"chain": t} for t in (after, before)]
    for device in partners:
        pl.semaphore_signal(barrier, inc=1, device_id=device, device_id_type=MESH)

    def load(source, target, index):
        copy = pltpu.make_async_copy(source, target, in_sem.at[index])
        copy.start()
        return copy

    wave_in = load(wave_hbm.at[0], x_v, 0)
    right_in = load(right_hbm.at[0], right_v, 1)
    diag_in = load(diag_hbm.at[0], diag_v, 2)
    hop_in = load(hop_hbm, hop_s, 3)

    def piece(s):
        return s // 2, pl.ds((s % 2) * (BS // 2), BS // 2)

    l_copies = []
    for s in range(4):
        p, rows = piece(s)
        l_copies.append(pltpu.make_async_remote_copy(
            src_ref=left_hbm.at[0, p, rows], dst_ref=left_v.at[p, rows],
            send_sem=l_send.at[s], recv_sem=l_recv.at[s], device_id={"chain": after}, device_id_type=MESH))

    def exchange(k, q):
        buf = bufs[k * NCH + q]
        copies = []
        for way, (slot, target) in enumerate(((0, up), (2, down))):
            copies.append(pltpu.make_async_remote_copy(
                src_ref=buf.at[1], dst_ref=buf.at[slot], send_sem=x_send.at[k, q, way], recv_sem=x_recv.at[k, q, way],
                device_id={"block": target}, device_id_type=MESH))
        return copies

    moves = [[exchange(k, q) for q in range(NCH)] for k in range(ITERS)]

    def columns(q):
        return pl.ds(q * CW, CW)

    wave_in.wait()
    for q in range(NCH):
        bufs[q][1] = x_v[:, columns(q)].astype(BF16)
    pl.semaphore_wait(barrier, len(partners))
    for copy in l_copies:
        copy.start()
    for q in range(NCH):
        for copy in moves[0][q]:
            copy.start()

    hop_in.wait()
    hops = [hop_s[p] for p in range(2)]
    right_in.wait()
    for p in range(2):
        source = j + hops[p] - 1
        inside = jnp.logical_and(source >= 0, source < nblk)
        rights = right_v[p].astype(F32) * jnp.where(inside, 1.0, 0.0).astype(F32)
        rt_v[p] = rights.T.astype(BF16)
    diag_in.wait()

    def prepare(shift):
        squares = jnp.zeros((8, CW), F32)
        for q in range(NCH):
            x = x_v[:, columns(q)]
            known = diag_v[:, columns(q)].astype(F32) * x
            c_v[:, columns(q)] = known
            b_v[:, columns(q)] = (1.0 + RATE * shift) * x - RATE * known
            squares += fold(x * x)
        return squares

    def update(energy, shift):
        squares = jnp.zeros((8, CW), F32)
        gap = RATE * (energy - shift)
        for q in range(NCH):
            x = x_v[:, columns(q)]
            x = x - RATE * (im_v[:, columns(q)] - energy * x)
            known = diag_v[:, columns(q)].astype(F32) * x + gap * dprev_v[:, columns(q)]
            x_v[:, columns(q)] = x
            c_v[:, columns(q)] = known
            b_v[:, columns(q)] = (1.0 + RATE * energy) * x - RATE * known
            squares += fold(x * x)
        return squares, gap

    def sums_start(k, product, squares):
        xpart[k, xi, 0:1] = jnp.sum(product, axis=0, keepdims=True)
        xpart[k, xi, 1:2] = jnp.sum(squares, axis=0, keepdims=True)
        copies = []
        for d, target in enumerate(x_others):
            copies.append(pltpu.make_async_remote_copy(
                src_ref=xpart.at[k, xi], dst_ref=xpart.at[k, xi], send_sem=s1_send.at[k, d], recv_sem=s1_recv.at[k, xi],
                device_id={"block": target}, device_id_type=MESH))
        for copy in copies:
            copy.start()
        return copies

    def sums_middle(k):
        for slot in x_slots:
            pltpu.make_async_copy(xpart.at[k, slot], xpart.at[k, slot], s1_recv.at[k, slot]).wait()
        total = xpart[k, 0]
        for slot in range(1, XG):
            total += xpart[k, slot]
        zpart[k, zi] = total
        copies = []
        for d, target in enumerate(z_others):
            copies.append(pltpu.make_async_remote_copy(
                src_ref=zpart.at[k, zi], dst_ref=zpart.at[k, zi], send_sem=s2_send.at[k, d], recv_sem=s2_recv.at[k, zi],
                device_id={"block": target}, device_id_type=MESH))
        for copy in copies:
            copy.start()
        return copies

    def sums_end(k):
        for slot in z_slots:
            pltpu.make_async_copy(zpart.at[k, slot], zpart.at[k, slot], s2_recv.at[k, slot]).wait()
        total = zpart[k, 0]
        for slot in range(1, zg):
            total += zpart[k, slot]
        total = jnp.sum(total, axis=1, keepdims=True)
        energy = total[0:1] / total[1:2]
        en_ref[0:1, k:k + 1] = energy
        return energy

    def arrived(k, q):
        for copy in moves[k][q]:
            copy.wait_recv()

    pending = []
    shift = FIRST_SHIFT
    gap = None
    squares = prepare(shift)
    for k in range(ITERS):
        last = None
        if k == 0:
            for s in range(NCH):
                arrived(0, s)
                l_copies[s].wait_recv()
                for t in range(s + 1):
                    p, rows = piece(t)
                    firsts = range(s + 1) if t == s else [s]
                    first = [dot(left_v[p, rows], bufs[q][hops[p]]).astype(BF16) for q in firsts]
                    first = jnp.concatenate(first, axis=1)
                    depth = pl.ds(firsts[0] * CW, len(firsts) * CW)
                    more = dot(first, rt_v[p, depth])
                    if s == 0:
                        d_v[rows] = more
                    elif t == s and s == 1:
                        d_v[rows] = more
                    else:
                        d_v[rows] = d_v[rows] + more
        else:
            for q in range(NCH):
                arrived(k, q)
                first = [dot(left_v[p], bufs[k * NCH + q][hops[p]]).astype(BF16) for p in range(2)]
                first = jnp.concatenate(first, axis=1)
                if q == NCH - 1:
                    last = first
                    break
                more = dot(first, jnp.concatenate([rt_v[p, columns(q)] for p in range(2)], axis=0))
                d_v[...] = more if q == 0 else d_v[...] + more
                if q == 0:
                    pending += sums_middle(k - 1)
                if q == 1:
                    energy = sums_end(k - 1)
                    squares, gap = update(energy, shift)
                    shift = energy
        for half in range(2):
            wide = pl.ds(half * 2 * CW, 2 * CW)
            if last is not None:
                rights = jnp.concatenate([rt_v[p, columns(NCH - 1), wide] for p in range(2)], axis=0)
                d_v[:, wide] = d_v[:, wide] + dot(last, rights)
            if k < ITERS - 1:
                for q in (2 * half, 2 * half + 1):
                    y = b_v[:, columns(q)] - RATE * d_v[:, columns(q)]
                    bufs[(k + 1) * NCH + q][1] = y.astype(BF16)
                    for copy in moves[k + 1][q]:
                        copy.start()
        product = jnp.zeros((8, CW), F32)
        for q in range(NCH):
            d = d_v[:, columns(q)]
            image = d + c_v[:, columns(q)]
            im_v[:, columns(q)] = image
            product += fold(x_v[:, columns(q)] * image)
        pending += sums_start(k, product, squares)
        if k < ITERS - 1:
            for q in range(NCH):
                d = d_v[:, columns(q)]
                dprev_v[:, columns(q)] = d if gap is None else d + gap * dprev_v[:, columns(q)]

    pending += sums_middle(ITERS - 1)
    energy = sums_end(ITERS - 1)
    outs = []
    for q in range(NCH):
        x = x_v[:, columns(q)]
        out_v[:, columns(q)] = x - RATE * (im_v[:, columns(q)] - energy * x)
    out = pltpu.make_async_copy(out_v, out_hbm.at[0], out_sem)
    out.start()
    for copy in pending + l_copies + [m for step in moves for pair in step for m in pair]:
        copy.wait_send()
    out.wait()


def shards(wave, diagonal, left_env, right_env, pair_hop, segs, nblk):
    zg = nblk // XG
    dma = pltpu.SemaphoreType.DMA
    square = pltpu.VMEM((BS, BS), F32)
    anywhere = pl.BlockSpec(memory_space=pl.ANY)
    return pl.pallas_call(
        functools.partial(kernel, segs, nblk),
        out_shape=(
            jax.ShapeDtypeStruct((1, BS, BS), F32),
            jax.ShapeDtypeStruct((1, ITERS), F32),
        ),
        in_specs=[anywhere] * 5,
        out_specs=(anywhere, pl.BlockSpec(memory_space=pltpu.VMEM)),
        scratch_shapes=[pltpu.VMEM((3, BS, CW), BF16)] * (ITERS * NCH) + [
            pltpu.SMEM((2,), jnp.int32),
            square,
            pltpu.VMEM((BS, BS), BF16),
            pltpu.VMEM((2, BS, BS), BF16),
            pltpu.VMEM((2, BS, BS), BF16),
            pltpu.VMEM((2, BS, BS), BF16),
            square, square, square, square, square, square,
            pltpu.VMEM((ITERS, XG, 2, 128), F32),
            pltpu.VMEM((ITERS, zg, 2, 128), F32),
            dma((4,)),
            dma(()),
            dma((4,)),
            dma((4,)),
            dma((ITERS, NCH, 2)),
            dma((ITERS, NCH, 2)),
            dma((ITERS, XG - 1)),
            dma((ITERS, XG)),
            dma((ITERS, max(zg - 1, 1))),
            dma((ITERS, zg)),
        ],
        compiler_params=pltpu.CompilerParams(
            collective_id=0, has_side_effects=True, vmem_limit_bytes=48 * 2 ** 20),
        cost_estimate=pl.CostEstimate(flops=ITERS * 8 * BS ** 3, bytes_accessed=9 * 2 ** 19, transcendentals=0),
    )(pair_hop, wave, diagonal, left_env, right_env)


def solution(mesh):
    placed = (
        P("chain", "block", None),
        P("chain", "block", None),
        P("chain", "block", None, None),
        P("chain", "block", None, None),
        P("block"),
    )
    return jax.shard_map(
        functools.partial(shards, segs=mesh.shape["chain"], nblk=mesh.shape["block"]),
        mesh=mesh,
        in_specs=placed,
        out_specs=(P("chain", "block", None), P("chain", None)),
        check_vma=False,
    )
```

```python
import functools

import jax
import jax.numpy as jnp
from jax import lax
from jax.experimental import pallas as pl
from jax.experimental.pallas import tpu as pltpu
from jax.sharding import PartitionSpec as P

MESH = pl.DeviceIdType.MESH
BS = 512
ITERS = 3
RATE = 0.3
SHIFT = 1.5
PAIRS = ((0, 0), (0, 1), (1, 1), (0, 2), (1, 2), (2, 2), (0, 3), (1, 3), (2, 3))
NCH = 4
CW = BS // NCH
XG = 4
F32 = jnp.float32
BF16 = jnp.bfloat16


def dot(a, b):
    return jnp.dot(a, b, preferred_element_type=F32)


def fold(values):
    return jnp.sum(values.reshape(BS // 8, 8, CW), axis=0)


def kernel(segs, nblk, *refs):
    (hop_hbm, wave_hbm, diag_hbm, left_hbm, right_hbm, out_ref, en_ref) = refs[:7]
    ys = refs[7:11]
    refs = refs[11:]
    bufs = refs[: ITERS * NCH]
    refs = refs[ITERS * NCH:]
    (hop_s, diag_v, right_v, left_v, rt_v, d_v, m_v,
     parts, in_sem, l_send, l_recv, x_send, x_recv, sum_sems, near_sem) = refs

    zg = nblk // XG
    c = lax.axis_index("chain")
    j = lax.axis_index("block")
    zi, xi = j // XG, j % XG
    up, down = (j + 1) % nblk, (j + nblk - 1) % nblk
    after, before = (c + 1) % segs, (c + segs - 1) % segs
    even = c % 2 == 0

    def block_at(dz, dx):
        return {"block": (zi + dz) % zg * XG + (xi + dx) % XG}

    def far(offset):
        dz, dx = offset
        return min(dz, zg - dz) + min(dx, XG - dx)

    others = [(dz, dx) for dz in range(zg) for dx in range(XG) if (dz, dx) != (0, 0)]
    others = sorted(others, key=far, reverse=True)

    barrier = pltpu.get_barrier_semaphore()
    partners = [{"block": up}, {"block": down}] + [block_at(0, dx) for dx in range(1, XG)]
    partners += [block_at(1, 0), block_at(zg - 1, 0), {"chain": after}, {"chain": before}]
    for device in partners:
        pl.semaphore_signal(barrier, inc=1, device_id=device, device_id_type=MESH)

    reaches = [1 << r for r in range(zg.bit_length() - 1)]

    def near_start(r):
        for dz in {reaches[r], zg - reaches[r]}:
            pl.semaphore_signal(near_sem.at[r], inc=1, device_id=block_at(dz, 0), device_id_type=MESH)

    def near_next(r):
        if r < len(reaches):
            pl.semaphore_wait(near_sem.at[r], len({reaches[r], zg - reaches[r]}))
        if r + 1 < len(reaches):
            near_start(r + 1)

    def load(source, target, index):
        copy = pltpu.make_async_copy(source, target, in_sem.at[index])
        copy.start()
        return copy

    def columns(q):
        return pl.ds(q * CW, CW)

    wave_in = [load(wave_hbm.at[0, :, columns(q)], ys[0].at[:, columns(q)], q) for q in range(NCH)]
    right_in = load(right_hbm.at[0], right_v, NCH)
    diag_in = load(diag_hbm.at[0], diag_v, NCH + 1)
    hop_in = load(hop_hbm, hop_s, NCH + 2)

    def piece(s):
        return s // 2, pl.ds((s % 2) * (BS // 2), BS // 2)

    l_copies = []
    for s in range(4):
        p, rows = piece(s)
        l_copies.append(pltpu.make_async_remote_copy(
            src_ref=left_hbm.at[0, p, rows], dst_ref=left_v.at[p, rows],
            send_sem=l_send.at[s], recv_sem=l_recv.at[s], device_id={"chain": after}, device_id_type=MESH))

    def exchange(k, q):
        buf = bufs[k * NCH + q]
        copies = []
        for way, (slot, target) in enumerate(((0, up), (2, down))):
            copies.append(pltpu.make_async_remote_copy(
                src_ref=buf.at[1], dst_ref=buf.at[slot], send_sem=x_send.at[k, q, way], recv_sem=x_recv.at[k, q, way],
                device_id={"block": target}, device_id_type=MESH))
        return copies

    moves = [[exchange(k, q) for q in range(NCH)] for k in range(ITERS)]

    pl.semaphore_wait(barrier, len(partners))
    for copy in l_copies:
        copy.start()
    for q in range(NCH):
        wave_in[q].wait()
        bufs[q][1] = ys[0][:, columns(q)].astype(BF16)
        for copy in moves[0][q]:
            copy.start()
    near_start(0)

    hop_in.wait()
    hops = [hop_s[p] for p in range(2)]
    right_in.wait()
    for p in range(2):
        source = j + hops[p] - 1
        inside = jnp.logical_and(source >= 0, source < nblk)
        rights = right_v[p].astype(F32) * jnp.where(inside, 1.0, 0.0).astype(F32)
        rt_v[p] = rights.T.astype(BF16)
    diag_in.wait()

    for q in range(NCH):
        m_v[:, columns(q)] = (1.0 + RATE * SHIFT) - RATE * diag_v[:, columns(q)].astype(F32)

    lane = lax.broadcasted_iota(jnp.int32, (1, CW), 1)

    def inner(a, b):
        total = jnp.zeros((8, CW), F32)
        for q in range(NCH):
            total += fold(ys[a][:, columns(q)] * ys[b][:, columns(q)])
        return total

    def placed(pair, total):
        total = jnp.sum(jnp.sum(total, axis=0, keepdims=True), axis=1, keepdims=True)
        return jnp.where(lane == PAIRS.index(pair), total, 0.0)

    every = parts.at[pl.ds(0, nblk - 1)]

    def sums_start(row):
        parts[j] = row
        for dz, dx in others:
            pltpu.make_async_remote_copy(
                src_ref=parts.at[j], dst_ref=parts.at[j], send_sem=sum_sems.at[0], recv_sem=sum_sems.at[1],
                device_id=block_at(dz, dx), device_id_type=MESH).start()

    def arrived(k, q):
        for copy in moves[k][q]:
            copy.wait_recv()

    def first_terms(t, chunks, begin=False):
        p, rows = piece(t)
        first = [dot(left_v[p, rows], bufs[q][hops[p]]).astype(BF16) for q in chunks]
        first = jnp.concatenate(first, axis=1)
        more = dot(first, rt_v[p, pl.ds(chunks[0] * CW, len(chunks) * CW)])
        d_v[rows] = more if begin else d_v[rows] + more

    row = jnp.zeros((1, CW), F32)
    last_sums = [jnp.zeros((8, CW), F32)] * ITERS
    for k in range(ITERS):
        last = None
        if k == 0:
            for s in range(NCH - 1):
                arrived(0, s)
                l_copies[s].wait_recv()
                near_next(s)
                for t in range(s + 1):
                    first_terms(t, range(s + 1) if t == s else [s], t == s and s < 2)

            @pl.when(even)
            def _():
                arrived(0, NCH - 1)
                for t in range(NCH - 1):
                    first_terms(t, [NCH - 1])
                l_copies[NCH - 1].wait_recv()
                first_terms(NCH - 1, range(NCH))

            @pl.when(jnp.logical_not(even))
            def _():
                l_copies[NCH - 1].wait_recv()
                first_terms(NCH - 1, range(NCH - 1))
                arrived(0, NCH - 1)
                for t in range(NCH):
                    first_terms(t, [NCH - 1])

        else:
            for q in range(NCH):
                arrived(k, q)
                first = [dot(left_v[p], bufs[k * NCH + q][hops[p]]).astype(BF16) for p in range(2)]
                first = jnp.concatenate(first, axis=1)
                if q == NCH - 1:
                    last = first
                    break
                more = dot(first, jnp.concatenate([rt_v[p, columns(q)] for p in range(2)], axis=0))
                d_v[...] = more if q == 0 else d_v[...] + more
        for half in range(2):
            wide = pl.ds(half * 2 * CW, 2 * CW)
            if last is not None:
                rights = jnp.concatenate([rt_v[p, columns(NCH - 1), wide] for p in range(2)], axis=0)
                d_v[:, wide] = d_v[:, wide] + dot(last, rights)
            for q in (2 * half, 2 * half + 1):
                y = m_v[:, columns(q)] * ys[k][:, columns(q)] - RATE * d_v[:, columns(q)]
                ys[k + 1][:, columns(q)] = y
                if k < ITERS - 1:
                    bufs[(k + 1) * NCH + q][1] = y.astype(BF16)
                    for copy in moves[k + 1][q]:
                        copy.start()
                else:
                    for a in range(ITERS):
                        last_sums[a] += fold(ys[a][:, columns(q)] * y)
        if k < ITERS - 1:
            for pair in PAIRS:
                if pair[1] == k + 1 or (k == 0 and pair == (0, 0)):
                    row = row + placed(pair, inner(*pair))
    for r in range(NCH - 1, len(reaches)):
        near_next(r)
    for a in range(ITERS):
        row = row + placed((a, ITERS), last_sums[a])
    sums_start(row)
    for copy in l_copies + [m for step in moves for pair in step for m in pair]:
        copy.wait_send()
    pltpu.make_async_copy(every, every, sum_sems.at[1]).wait()
    total = jnp.sum(parts[...], axis=0)
    g = {}
    for i, (a, b) in enumerate(PAIRS):
        g[a, b] = total[0:1, i:i + 1]
    b0 = 1.0 - g[0, 1] / g[0, 0]
    squares = g[1, 1] + b0 * (2.0 * g[0, 1] + b0 * g[0, 0])
    b1 = 1.0 - (g[1, 2] + b0 * (g[1, 1] + g[0, 2] + b0 * g[0, 1])) / squares
    s, t = b0 + b1, b0 * b1
    squares = g[2, 2] + s * (2.0 * g[1, 2] + s * g[1, 1] + 2.0 * t * g[0, 1]) + t * (2.0 * g[0, 2] + t * g[0, 0])
    product = g[2, 3] + s * (g[2, 2] + g[1, 3] + s * g[1, 2] + t * g[1, 1])
    product = product + t * (g[1, 2] + g[0, 3] + s * g[0, 2] + t * g[0, 1])
    b2 = 1.0 - product / squares
    for k, b in enumerate((b0, b1, b2)):
        en_ref[0:1, k:k + 1] = SHIFT + b * (1.0 / RATE)
    one, two, three = s + b2, t + s * b2, t * b2
    for q in range(NCH):
        known = one * ys[2][:, columns(q)] + two * ys[1][:, columns(q)] + three * ys[0][:, columns(q)]
        out_ref[0, :, columns(q)] = ys[3][:, columns(q)] + known
    pltpu.make_async_copy(every, every, sum_sems.at[0]).wait()


def shards(wave, diagonal, left_env, right_env, pair_hop, segs, nblk):
    zg = nblk // XG
    dma = pltpu.SemaphoreType.DMA
    square = pltpu.VMEM((BS, BS), F32)
    vmem = pl.BlockSpec(memory_space=pltpu.VMEM)
    given = [pltpu.with_memory_space_constraint(a, pltpu.HBM) for a in (pair_hop, wave, diagonal, left_env, right_env)]
    return pl.pallas_call(
        functools.partial(kernel, segs, nblk),
        out_shape=(
            jax.ShapeDtypeStruct((1, BS, BS), F32),
            jax.ShapeDtypeStruct((1, ITERS), F32),
        ),
        in_specs=[pl.BlockSpec(memory_space=pl.ANY)] * 5,
        out_specs=(vmem, vmem),
        scratch_shapes=[square] * (ITERS + 1) + [pltpu.VMEM((3, BS, CW), BF16)] * (ITERS * NCH) + [
            pltpu.SMEM((2,), jnp.int32),
            pltpu.VMEM((BS, BS), BF16),
            pltpu.VMEM((2, BS, BS), BF16),
            pltpu.VMEM((2, BS, BS), BF16),
            pltpu.VMEM((2, BS, BS), BF16),
            square, square,
            pltpu.VMEM((nblk, 1, CW), F32),
            dma((NCH + 3,)),
            dma((4,)),
            dma((4,)),
            dma((ITERS, NCH, 2)),
            dma((ITERS, NCH, 2)),
            dma((2,)),
            pltpu.SemaphoreType.REGULAR((zg.bit_length() - 1,)),
        ],
        compiler_params=pltpu.CompilerParams(
            collective_id=0, has_side_effects=True, vmem_limit_bytes=48 * 2 ** 20),
        cost_estimate=pl.CostEstimate(flops=ITERS * 8 * BS ** 3, bytes_accessed=9 * 2 ** 19, transcendentals=0),
    )(*given)


def solution(mesh):
    placed = (
        P("chain", "block", None),
        P("chain", "block", None),
        P("chain", "block", None, None),
        P("chain", "block", None, None),
        P("block"),
    )
    return jax.shard_map(
        functools.partial(shards, segs=mesh.shape["chain"], nblk=mesh.shape["block"]),
        mesh=mesh,
        in_specs=placed,
        out_specs=(P("chain", "block", None), P("chain", None)),
        check_vma=False,
    )
```

```python
import functools

import jax
import jax.numpy as jnp
from jax import lax
from jax.experimental import pallas as pl
from jax.experimental.pallas import tpu as pltpu
from jax.sharding import PartitionSpec as P

MESH = pl.DeviceIdType.MESH
BS = 512
ITERS = 3
RATE = 0.3
SHIFT = 1.5
PAIRS = ((0, 0), (0, 1), (1, 1), (0, 2), (1, 2), (2, 2), (0, 3), (1, 3), (2, 3))
NCH = 4
CW = BS // NCH
XG = 4
F32 = jnp.float32
BF16 = jnp.bfloat16


def dot(a, b):
    return jnp.dot(a, b, preferred_element_type=F32)


def fold(values):
    return jnp.sum(values.reshape(BS // 8, 8, CW), axis=0)


def kernel(segs, nblk, *refs):
    (hop_hbm, wave_hbm, diag_hbm, left_hbm, right_hbm, out_ref, en_ref) = refs[:7]
    ys = refs[7:11]
    refs = refs[11:]
    bufs = refs[: ITERS * NCH]
    refs = refs[ITERS * NCH:]
    (hop_s, diag_v, right_v, left_v, rt_v, d_v, m_v,
     parts, in_sem, l_send, l_recv, x_send, x_recv, sum_sems, near_sem) = refs

    zg = nblk // XG
    c = lax.axis_index("chain")
    j = lax.axis_index("block")
    zi, xi = j // XG, j % XG
    up, down = (j + 1) % nblk, (j + nblk - 1) % nblk
    after, before = (c + 1) % segs, (c + segs - 1) % segs
    even = c % 2 == 0

    def block_at(dz, dx):
        return {"block": (zi + dz) % zg * XG + (xi + dx) % XG}

    def far(offset):
        dz, dx = offset
        return min(dz, zg - dz) + min(dx, XG - dx)

    others = [(dz, dx) for dz in range(zg) for dx in range(XG) if (dz, dx) != (0, 0)]
    others = sorted(others, key=far, reverse=True)

    barrier = pltpu.get_barrier_semaphore()
    partners = [{"block": up}, {"block": down}] + [block_at(0, dx) for dx in range(1, XG)]
    partners += [block_at(1, 0), block_at(zg - 1, 0), {"chain": after}, {"chain": before}]
    for device in partners:
        pl.semaphore_signal(barrier, inc=1, device_id=device, device_id_type=MESH)

    reaches = [1 << r for r in range(zg.bit_length() - 1)]

    def near_start(r):
        for dz in {reaches[r], zg - reaches[r]}:
            pl.semaphore_signal(near_sem.at[r], inc=1, device_id=block_at(dz, 0), device_id_type=MESH)

    def near_next(r):
        if r < len(reaches):
            pl.semaphore_wait(near_sem.at[r], len({reaches[r], zg - reaches[r]}))
        if r + 1 < len(reaches):
            near_start(r + 1)

    def load(source, target, index):
        copy = pltpu.make_async_copy(source, target, in_sem.at[index])
        copy.start()
        return copy

    def columns(q):
        return pl.ds(q * CW, CW)

    wave_in = [load(wave_hbm.at[0, :, columns(q)], ys[0].at[:, columns(q)], q) for q in range(NCH)]
    right_in = load(right_hbm.at[0], right_v, NCH)
    diag_in = load(diag_hbm.at[0], diag_v, NCH + 1)
    hop_in = load(hop_hbm, hop_s, NCH + 2)

    def piece(s):
        return s // 2, pl.ds((s % 2) * (BS // 2), BS // 2)

    l_copies = []
    for s in range(4):
        p, rows = piece(s)
        l_copies.append(pltpu.make_async_remote_copy(
            src_ref=left_hbm.at[0, p, rows], dst_ref=left_v.at[p, rows],
            send_sem=l_send.at[s], recv_sem=l_recv.at[s], device_id={"chain": after}, device_id_type=MESH))

    def exchange(k, q):
        buf = bufs[k * NCH + q]
        copies = []
        for way, (slot, target) in enumerate(((0, up), (2, down))):
            copies.append(pltpu.make_async_remote_copy(
                src_ref=buf.at[1], dst_ref=buf.at[slot], send_sem=x_send.at[k, q, way], recv_sem=x_recv.at[k, q, way],
                device_id={"block": target}, device_id_type=MESH))
        return copies

    moves = [[exchange(k, q) for q in range(NCH)] for k in range(ITERS)]

    pl.semaphore_wait(barrier, len(partners))
    for copy in l_copies:
        copy.start()

    def send_first(chunks):
        for q in chunks:
            for copy in moves[0][q]:
                copy.start()

    for q in range(NCH):
        wave_in[q].wait()
        bufs[q][1] = ys[0][:, columns(q)].astype(BF16)
        if q == 0:
            send_first([q])
        else:
            pl.when(jnp.logical_not(even))(functools.partial(send_first, [q]))
    near_start(0)

    hop_in.wait()
    hops = [hop_s[p] for p in range(2)]
    right_in.wait()
    for p in range(2):
        source = j + hops[p] - 1
        inside = jnp.logical_and(source >= 0, source < nblk)
        rights = right_v[p].astype(F32) * jnp.where(inside, 1.0, 0.0).astype(F32)
        rt_v[p] = rights.T.astype(BF16)
    diag_in.wait()

    l_copies[0].wait_recv()
    pl.when(even)(functools.partial(send_first, range(1, NCH)))

    for q in range(NCH):
        m_v[:, columns(q)] = (1.0 + RATE * SHIFT) - RATE * diag_v[:, columns(q)].astype(F32)

    lane = lax.broadcasted_iota(jnp.int32, (1, CW), 1)

    def inner(a, b):
        total = jnp.zeros((8, CW), F32)
        for q in range(NCH):
            total += fold(ys[a][:, columns(q)] * ys[b][:, columns(q)])
        return total

    def placed(pair, total):
        total = jnp.sum(jnp.sum(total, axis=0, keepdims=True), axis=1, keepdims=True)
        return jnp.where(lane == PAIRS.index(pair), total, 0.0)

    every = parts.at[pl.ds(0, nblk - 1)]

    def sums_start(row):
        parts[j] = row
        for dz, dx in others:
            pltpu.make_async_remote_copy(
                src_ref=parts.at[j], dst_ref=parts.at[j], send_sem=sum_sems.at[0], recv_sem=sum_sems.at[1],
                device_id=block_at(dz, dx), device_id_type=MESH).start()

    def arrived(k, q):
        for copy in moves[k][q]:
            copy.wait_recv()

    def first_terms(t, chunks, begin=False):
        p, rows = piece(t)
        first = [dot(left_v[p, rows], bufs[q][hops[p]]).astype(BF16) for q in chunks]
        first = jnp.concatenate(first, axis=1)
        more = dot(first, rt_v[p, pl.ds(chunks[0] * CW, len(chunks) * CW)])
        d_v[rows] = more if begin else d_v[rows] + more

    row = jnp.zeros((1, CW), F32)
    last_sums = [jnp.zeros((8, CW), F32)] * ITERS
    for k in range(ITERS):
        last = None
        if k == 0:
            for s in range(NCH - 1):
                arrived(0, s)
                if s > 0:
                    l_copies[s].wait_recv()
                near_next(s)
                for t in range(s + 1):
                    first_terms(t, range(s + 1) if t == s else [s], t == s and s < 2)

            @pl.when(even)
            def _():
                arrived(0, NCH - 1)
                for t in range(NCH - 1):
                    first_terms(t, [NCH - 1])
                l_copies[NCH - 1].wait_recv()
                first_terms(NCH - 1, range(NCH))

            @pl.when(jnp.logical_not(even))
            def _():
                l_copies[NCH - 1].wait_recv()
                first_terms(NCH - 1, range(NCH - 1))
                arrived(0, NCH - 1)
                for t in range(NCH):
                    first_terms(t, [NCH - 1])

        else:
            for q in range(NCH):
                arrived(k, q)
                first = [dot(left_v[p], bufs[k * NCH + q][hops[p]]).astype(BF16) for p in range(2)]
                first = jnp.concatenate(first, axis=1)
                if q == NCH - 1:
                    last = first
                    break
                more = dot(first, jnp.concatenate([rt_v[p, columns(q)] for p in range(2)], axis=0))
                d_v[...] = more if q == 0 else d_v[...] + more
        for half in range(2):
            wide = pl.ds(half * 2 * CW, 2 * CW)
            if last is not None:
                rights = jnp.concatenate([rt_v[p, columns(NCH - 1), wide] for p in range(2)], axis=0)
                d_v[:, wide] = d_v[:, wide] + dot(last, rights)
            for q in (2 * half, 2 * half + 1):
                y = m_v[:, columns(q)] * ys[k][:, columns(q)] - RATE * d_v[:, columns(q)]
                ys[k + 1][:, columns(q)] = y
                if k < ITERS - 1:
                    bufs[(k + 1) * NCH + q][1] = y.astype(BF16)
                    for copy in moves[k + 1][q]:
                        copy.start()
                else:
                    for a in range(ITERS):
                        last_sums[a] += fold(ys[a][:, columns(q)] * y)
        if k < ITERS - 1:
            for pair in PAIRS:
                if pair[1] == k + 1 or (k, pair) == (0, (0, 0)):
                    row = row + placed(pair, inner(*pair))
    for r in range(NCH - 1, len(reaches)):
        near_next(r)
    for a in range(ITERS):
        row = row + placed((a, ITERS), last_sums[a])
    sums_start(row)
    for copy in l_copies + [m for step in moves for pair in step for m in pair]:
        copy.wait_send()
    pltpu.make_async_copy(every, every, sum_sems.at[1]).wait()
    total = jnp.sum(parts[...], axis=0)
    g = {}
    for i, (a, b) in enumerate(PAIRS):
        g[a, b] = total[0:1, i:i + 1]
    b0 = 1.0 - g[0, 1] / g[0, 0]
    squares = g[1, 1] + b0 * (2.0 * g[0, 1] + b0 * g[0, 0])
    b1 = 1.0 - (g[1, 2] + b0 * (g[1, 1] + g[0, 2] + b0 * g[0, 1])) / squares
    s, t = b0 + b1, b0 * b1
    squares = g[2, 2] + s * (2.0 * g[1, 2] + s * g[1, 1] + 2.0 * t * g[0, 1]) + t * (2.0 * g[0, 2] + t * g[0, 0])
    product = g[2, 3] + s * (g[2, 2] + g[1, 3] + s * g[1, 2] + t * g[1, 1])
    product = product + t * (g[1, 2] + g[0, 3] + s * g[0, 2] + t * g[0, 1])
    b2 = 1.0 - product / squares
    for k, b in enumerate((b0, b1, b2)):
        en_ref[0:1, k:k + 1] = SHIFT + b * (1.0 / RATE)
    one, two, three = s + b2, t + s * b2, t * b2
    for q in range(NCH):
        known = one * ys[2][:, columns(q)] + two * ys[1][:, columns(q)] + three * ys[0][:, columns(q)]
        out_ref[0, :, columns(q)] = ys[3][:, columns(q)] + known
    pltpu.make_async_copy(every, every, sum_sems.at[0]).wait()


def shards(wave, diagonal, left_env, right_env, pair_hop, segs, nblk):
    zg = nblk // XG
    dma = pltpu.SemaphoreType.DMA
    square = pltpu.VMEM((BS, BS), F32)
    vmem = pl.BlockSpec(memory_space=pltpu.VMEM)
    given = [pltpu.with_memory_space_constraint(a, pltpu.HBM) for a in (pair_hop, wave, diagonal, left_env, right_env)]
    return pl.pallas_call(
        functools.partial(kernel, segs, nblk),
        out_shape=(
            jax.ShapeDtypeStruct((1, BS, BS), F32),
            jax.ShapeDtypeStruct((1, ITERS), F32),
        ),
        in_specs=[pl.BlockSpec(memory_space=pl.ANY)] * 5,
        out_specs=(vmem, vmem),
        scratch_shapes=[square] * (ITERS + 1) + [pltpu.VMEM((3, BS, CW), BF16)] * (ITERS * NCH) + [
            pltpu.SMEM((2,), jnp.int32),
            pltpu.VMEM((BS, BS), BF16),
            pltpu.VMEM((2, BS, BS), BF16),
            pltpu.VMEM((2, BS, BS), BF16),
            pltpu.VMEM((2, BS, BS), BF16),
            square, square,
            pltpu.VMEM((nblk, 1, CW), F32),
            dma((NCH + 3,)),
            dma((4,)),
            dma((4,)),
            dma((ITERS, NCH, 2)),
            dma((ITERS, NCH, 2)),
            dma((2,)),
            pltpu.SemaphoreType.REGULAR((zg.bit_length() - 1,)),
        ],
        compiler_params=pltpu.CompilerParams(
            collective_id=0, has_side_effects=True, vmem_limit_bytes=48 * 2 ** 20),
        cost_estimate=pl.CostEstimate(flops=ITERS * 8 * BS ** 3, bytes_accessed=9 * 2 ** 19, transcendentals=0),
    )(*given)


def solution(mesh):
    placed = (
        P("chain", "block", None),
        P("chain", "block", None),
        P("chain", "block", None, None),
        P("chain", "block", None, None),
        P("block"),
    )
    return jax.shard_map(
        functools.partial(shards, segs=mesh.shape["chain"], nblk=mesh.shape["block"]),
        mesh=mesh,
        in_specs=placed,
        out_specs=(P("chain", "block", None), P("chain", None)),
        check_vma=False,
    )
```

```python
import functools

import jax
import jax.numpy as jnp
from jax import lax
from jax.experimental import pallas as pl
from jax.experimental.pallas import tpu as pltpu
from jax.sharding import PartitionSpec as P

MESH = pl.DeviceIdType.MESH
BS = 512
ITERS = 3
RATE = 0.3
SHIFT = 1.5
PAIRS = ((0, 0), (0, 1), (1, 1), (0, 2), (1, 2), (2, 2), (0, 3), (1, 3), (2, 3))
NCH = 4
CW = BS // NCH
XG = 4
F32 = jnp.float32
BF16 = jnp.bfloat16


def dot(a, b):
    return jnp.dot(a, b, preferred_element_type=F32)


def fold(values):
    return jnp.sum(values.reshape(BS // 8, 8, CW), axis=0)


def kernel(segs, nblk, *refs):
    (hop_hbm, wave_hbm, diag_hbm, left_hbm, right_hbm, out_ref, en_ref) = refs[:7]
    ys = refs[7:11]
    refs = refs[11:]
    bufs = refs[: ITERS * NCH]
    refs = refs[ITERS * NCH:]
    (hop_s, diag_v, right_v, left_v, rt_v, d_v, m_v,
     parts, in_sem, l_send, l_recv, x_send, x_recv, sum_sems, near_sem) = refs

    zg = nblk // XG
    c = lax.axis_index("chain")
    j = lax.axis_index("block")
    zi, xi = j // XG, j % XG
    up, down = (j + 1) % nblk, (j + nblk - 1) % nblk
    after, before = (c + 1) % segs, (c + segs - 1) % segs
    even = c % 2 == 0

    def block_at(dz, dx):
        return {"block": (zi + dz) % zg * XG + (xi + dx) % XG}

    barrier = pltpu.get_barrier_semaphore()
    partners = [{"block": up}, {"block": down}] + [block_at(0, dx) for dx in range(1, XG)]
    partners += [block_at(1, 0), block_at(zg - 1, 0), {"chain": after}, {"chain": before}]
    for device in partners:
        pl.semaphore_signal(barrier, inc=1, device_id=device, device_id_type=MESH)

    reaches = [1 << r for r in range(zg.bit_length() - 1)]

    def near_start(r):
        for dz in {reaches[r], zg - reaches[r]}:
            pl.semaphore_signal(near_sem.at[r], inc=1, device_id=block_at(dz, 0), device_id_type=MESH)

    def near_next(r):
        if r < len(reaches):
            pl.semaphore_wait(near_sem.at[r], len({reaches[r], zg - reaches[r]}))
        if r + 1 < len(reaches):
            near_start(r + 1)

    def load(source, target, index):
        copy = pltpu.make_async_copy(source, target, in_sem.at[index])
        copy.start()
        return copy

    def columns(q):
        return pl.ds(q * CW, CW)

    wave_in = [load(wave_hbm.at[0, :, columns(q)], ys[0].at[:, columns(q)], q) for q in range(NCH)]
    right_in = load(right_hbm.at[0], right_v, NCH)
    diag_in = load(diag_hbm.at[0], diag_v, NCH + 1)
    hop_in = load(hop_hbm, hop_s, NCH + 2)

    half = BS // 2
    pieces = [(0, 0, half), (0, half, half), (1, 0, half), (1, half, half - 64), (1, BS - 64, 64)]

    def piece(s):
        p, start, size = pieces[s]
        return p, pl.ds(start, size)

    l_copies = []
    for s in range(len(pieces)):
        p, rows = piece(s)
        l_copies.append(pltpu.make_async_remote_copy(
            src_ref=left_hbm.at[0, p, rows], dst_ref=left_v.at[p, rows],
            send_sem=l_send.at[s], recv_sem=l_recv.at[s], device_id={"chain": after}, device_id_type=MESH))

    def exchange(k, q):
        buf = bufs[k * NCH + q]
        copies = []
        for way, (slot, target) in enumerate(((0, up), (2, down))):
            copies.append(pltpu.make_async_remote_copy(
                src_ref=buf.at[1], dst_ref=buf.at[slot], send_sem=x_send.at[k, q, way], recv_sem=x_recv.at[k, q, way],
                device_id={"block": target}, device_id_type=MESH))
        return copies

    moves = [[exchange(k, q) for q in range(NCH)] for k in range(ITERS)]

    pl.semaphore_wait(barrier, len(partners))
    for copy in l_copies:
        copy.start()

    def send_first(chunks):
        for q in chunks:
            for copy in moves[0][q]:
                copy.start()

    for q in range(NCH):
        wave_in[q].wait()
        bufs[q][1] = ys[0][:, columns(q)].astype(BF16)
        if q == 0:
            send_first([q])
        else:
            pl.when(jnp.logical_not(even))(functools.partial(send_first, [q]))
    near_start(0)

    hop_in.wait()
    hops = [hop_s[p] for p in range(2)]
    right_in.wait()
    for p in range(2):
        source = j + hops[p] - 1
        inside = jnp.logical_and(source >= 0, source < nblk)
        rights = right_v[p].astype(F32) * jnp.where(inside, 1.0, 0.0).astype(F32)
        rt_v[p] = rights.T.astype(BF16)
    diag_in.wait()

    l_copies[0].wait_recv()
    pl.when(even)(functools.partial(send_first, range(1, NCH)))

    for q in range(NCH):
        m_v[:, columns(q)] = (1.0 + RATE * SHIFT) - RATE * diag_v[:, columns(q)].astype(F32)

    lane = lax.broadcasted_iota(jnp.int32, (1, CW), 1)

    def inner(a, b):
        total = jnp.zeros((8, CW), F32)
        for q in range(NCH):
            total += fold(ys[a][:, columns(q)] * ys[b][:, columns(q)])
        return total

    def placed(pair, total):
        total = jnp.sum(jnp.sum(total, axis=0, keepdims=True), axis=1, keepdims=True)
        return jnp.where(lane == PAIRS.index(pair), total, 0.0)

    every = parts.at[pl.ds(0, nblk - 1)]

    def sums_start(row):
        parts[j] = row
        for t in range(nblk - 1):
            other = t + (t >= j).astype(jnp.int32)
            pltpu.make_async_remote_copy(
                src_ref=parts.at[j], dst_ref=parts.at[j], send_sem=sum_sems.at[0], recv_sem=sum_sems.at[1],
                device_id={"block": other}, device_id_type=MESH).start()

    def arrived(k, q):
        for copy in moves[k][q]:
            copy.wait_recv()

    def first_terms(t, chunks, begin=False):
        p, rows = piece(t)
        first = [dot(left_v[p, rows], bufs[q][hops[p]]).astype(BF16) for q in chunks]
        first = jnp.concatenate(first, axis=1)
        more = dot(first, rt_v[p, pl.ds(chunks[0] * CW, len(chunks) * CW)])
        d_v[rows] = more if begin else d_v[rows] + more

    row = jnp.zeros((1, CW), F32)
    last_sums = [jnp.zeros((8, CW), F32)] * ITERS
    for k in range(ITERS):
        last = None
        if k == 0:
            for s in range(NCH - 1):
                arrived(0, s)
                if s > 0:
                    l_copies[s].wait_recv()
                near_next(s)
                for t in range(s + 1):
                    first_terms(t, range(s + 1) if t == s else [s], t == s and s < 2)

            @pl.when(even)
            def _():
                arrived(0, NCH - 1)
                for t in range(NCH - 1):
                    first_terms(t, [NCH - 1])
                for t in range(NCH - 1, len(pieces)):
                    l_copies[t].wait_recv()
                    first_terms(t, range(NCH))

            @pl.when(jnp.logical_not(even))
            def _():
                for t in range(NCH - 1, len(pieces)):
                    l_copies[t].wait_recv()
                    first_terms(t, range(NCH - 1))
                arrived(0, NCH - 1)
                for t in range(len(pieces)):
                    first_terms(t, [NCH - 1])

        else:
            for q in range(NCH):
                arrived(k, q)
                first = [dot(left_v[p], bufs[k * NCH + q][hops[p]]).astype(BF16) for p in range(2)]
                first = jnp.concatenate(first, axis=1)
                if q == NCH - 1:
                    last = first
                    break
                more = dot(first, jnp.concatenate([rt_v[p, columns(q)] for p in range(2)], axis=0))
                d_v[...] = more if q == 0 else d_v[...] + more
        for q in range(NCH):
            d = d_v[:, columns(q)]
            if last is not None:
                d = d + dot(last, jnp.concatenate([rt_v[p, columns(NCH - 1), columns(q)] for p in range(2)], axis=0))
            y = m_v[:, columns(q)] * ys[k][:, columns(q)] - RATE * d
            ys[k + 1][:, columns(q)] = y
            if k < ITERS - 1:
                bufs[(k + 1) * NCH + q][1] = y.astype(BF16)
                for copy in moves[k + 1][q]:
                    copy.start()
            else:
                for a in range(ITERS):
                    last_sums[a] += fold(ys[a][:, columns(q)] * y)
        if k < ITERS - 1:
            for pair in PAIRS:
                if pair[1] == k + 1 or (k, pair) == (0, (0, 0)):
                    row = row + placed(pair, inner(*pair))
    for r in range(NCH - 1, len(reaches)):
        near_next(r)
    for a in range(ITERS):
        row = row + placed((a, ITERS), last_sums[a])
    sums_start(row)
    for copy in l_copies + [m for step in moves for pair in step for m in pair]:
        copy.wait_send()
    pltpu.make_async_copy(every, every, sum_sems.at[1]).wait()
    total = jnp.sum(parts[...], axis=0)
    g = {}
    for i, (a, b) in enumerate(PAIRS):
        g[a, b] = total[0:1, i:i + 1]
    b0 = 1.0 - g[0, 1] / g[0, 0]
    squares = g[1, 1] + b0 * (2.0 * g[0, 1] + b0 * g[0, 0])
    b1 = 1.0 - (g[1, 2] + b0 * (g[1, 1] + g[0, 2] + b0 * g[0, 1])) / squares
    s, t = b0 + b1, b0 * b1
    squares = g[2, 2] + s * (2.0 * g[1, 2] + s * g[1, 1] + 2.0 * t * g[0, 1]) + t * (2.0 * g[0, 2] + t * g[0, 0])
    product = g[2, 3] + s * (g[2, 2] + g[1, 3] + s * g[1, 2] + t * g[1, 1])
    product = product + t * (g[1, 2] + g[0, 3] + s * g[0, 2] + t * g[0, 1])
    b2 = 1.0 - product / squares
    for k, b in enumerate((b0, b1, b2)):
        en_ref[0:1, k:k + 1] = SHIFT + b * (1.0 / RATE)
    one, two, three = s + b2, t + s * b2, t * b2
    for q in range(NCH):
        known = one * ys[2][:, columns(q)] + two * ys[1][:, columns(q)] + three * ys[0][:, columns(q)]
        out_ref[0, :, columns(q)] = ys[3][:, columns(q)] + known
    pltpu.make_async_copy(every, every, sum_sems.at[0]).wait()


def shards(wave, diagonal, left_env, right_env, pair_hop, segs, nblk):
    zg = nblk // XG
    dma = pltpu.SemaphoreType.DMA
    square = pltpu.VMEM((BS, BS), F32)
    vmem = pl.BlockSpec(memory_space=pltpu.VMEM)
    given = [pltpu.with_memory_space_constraint(a, pltpu.HBM) for a in (pair_hop, wave, diagonal, left_env, right_env)]
    return pl.pallas_call(
        functools.partial(kernel, segs, nblk),
        out_shape=(
            jax.ShapeDtypeStruct((1, BS, BS), F32),
            jax.ShapeDtypeStruct((1, ITERS), F32),
        ),
        in_specs=[pl.BlockSpec(memory_space=pl.ANY)] * 5,
        out_specs=(vmem, vmem),
        scratch_shapes=[square] * (ITERS + 1) + [pltpu.VMEM((3, BS, CW), BF16)] * (ITERS * NCH) + [
            pltpu.SMEM((2,), jnp.int32),
            pltpu.VMEM((BS, BS), BF16),
            pltpu.VMEM((2, BS, BS), BF16),
            pltpu.VMEM((2, BS, BS), BF16),
            pltpu.VMEM((2, BS, BS), BF16),
            square, square,
            pltpu.VMEM((nblk, 1, CW), F32),
            dma((NCH + 3,)),
            dma((5,)),
            dma((5,)),
            dma((ITERS, NCH, 2)),
            dma((ITERS, NCH, 2)),
            dma((2,)),
            pltpu.SemaphoreType.REGULAR((zg.bit_length() - 1,)),
        ],
        compiler_params=pltpu.CompilerParams(
            collective_id=0, has_side_effects=True, vmem_limit_bytes=48 * 2 ** 20),
        cost_estimate=pl.CostEstimate(flops=ITERS * 8 * BS ** 3, bytes_accessed=9 * 2 ** 19, transcendentals=0),
    )(*given)


def solution(mesh):
    placed = (
        P("chain", "block", None),
        P("chain", "block", None),
        P("chain", "block", None, None),
        P("chain", "block", None, None),
        P("block"),
    )
    return jax.shard_map(
        functools.partial(shards, segs=mesh.shape["chain"], nblk=mesh.shape["block"]),
        mesh=mesh,
        in_specs=placed,
        out_specs=(P("chain", "block", None), P("chain", None)),
        check_vma=False,
    )
```

```python
import functools

import jax
import jax.numpy as jnp
from jax import lax
from jax.experimental import pallas as pl
from jax.experimental.pallas import tpu as pltpu
from jax.sharding import PartitionSpec as P

MESH = pl.DeviceIdType.MESH
BS = 512
ITERS = 3
RATE = 0.3
SHIFT = 1.5
PAIRS = ((0, 0), (0, 1), (1, 1), (0, 2), (1, 2), (2, 2), (0, 3), (1, 3), (2, 3))
NCH = 4
CW = BS // NCH
XG = 4
F32 = jnp.float32
BF16 = jnp.bfloat16


def dot(a, b):
    return jnp.dot(a, b, preferred_element_type=F32)


def fold(values):
    return jnp.sum(values.reshape(BS // 8, 8, CW), axis=0)


def kernel(segs, nblk, *refs):
    (hop_hbm, wave_hbm, diag_hbm, left_hbm, right_hbm, out_ref, en_ref) = refs[:7]
    ys = refs[7:11]
    refs = refs[11:]
    bufs = refs[: ITERS * NCH]
    refs = refs[ITERS * NCH:]
    (hop_s, diag_v, right_v, left_v, rt_v, d_v, m_v,
     parts, in_sem, l_send, l_recv, x_send, x_recv, sum_sems, near_sem) = refs

    zg = nblk // XG
    c = lax.axis_index("chain")
    j = lax.axis_index("block")
    zi, xi = j // XG, j % XG
    up, down = (j + 1) % nblk, (j + nblk - 1) % nblk
    after, before = (c + 1) % segs, (c + segs - 1) % segs
    even = c % 2 == 0

    def block_at(dz, dx):
        return {"block": (zi + dz) % zg * XG + (xi + dx) % XG}

    def far(offset):
        dz, dx = offset
        return min(dz, zg - dz) + min(dx, XG - dx)

    others = [(dz, dx) for dz in range(zg) for dx in range(XG) if (dz, dx) != (0, 0)]
    others = sorted(others, key=far, reverse=True)

    has_up, has_down = j < nblk - 1, j > 0

    def one_if(condition):
        return jnp.where(condition, 1, 0)

    def signal(semaphore, device):
        pl.semaphore_signal(semaphore, inc=1, device_id=device, device_id_type=MESH)

    barrier = pltpu.get_barrier_semaphore()
    fixed = [block_at(0, dx) for dx in range(1, XG)] + [{"chain": after}, {"chain": before}]
    for device in fixed:
        signal(barrier, device)
    ends = [(has_up, {"block": up}), (has_down, {"block": down})]
    ends += [(zi < zg - 1, block_at(1, 0)), (zi > 0, block_at(zg - 1, 0))]
    for condition, device in ends:
        pl.when(condition)(functools.partial(signal, barrier, device))
    entered = len(fixed) + sum(one_if(condition) for condition, _ in ends)

    reaches = [1 << r for r in range(zg.bit_length() - 1)]

    def near_ends(r):
        reach = reaches[r]
        return [(zi < zg - reach, block_at(reach, 0)), (zi >= reach, block_at(zg - reach, 0))]

    def near_start(r):
        for condition, device in near_ends(r):
            pl.when(condition)(functools.partial(signal, near_sem.at[r], device))

    def near_next(r):
        if r < len(reaches):
            pl.semaphore_wait(near_sem.at[r], sum(one_if(condition) for condition, _ in near_ends(r)))
        if r + 1 < len(reaches):
            near_start(r + 1)

    def load(source, target, index):
        copy = pltpu.make_async_copy(source, target, in_sem.at[index])
        copy.start()
        return copy

    def columns(q):
        return pl.ds(q * CW, CW)

    wave_in = [load(wave_hbm.at[0, :, columns(q)], ys[0].at[:, columns(q)], q) for q in range(NCH)]
    right_in = load(right_hbm.at[0], right_v, NCH)
    diag_in = load(diag_hbm.at[0], diag_v, NCH + 1)
    hop_in = load(hop_hbm, hop_s, NCH + 2)

    def piece(s):
        return s // 2, pl.ds((s % 2) * (BS // 2), BS // 2)

    def left_copy(index, p, rows):
        return pltpu.make_async_remote_copy(
            src_ref=left_hbm.at[0, p, rows], dst_ref=left_v.at[p, rows],
            send_sem=l_send.at[index], recv_sem=l_recv.at[index], device_id={"chain": after}, device_id_type=MESH)

    head = 32
    l_head = left_copy(4, 0, pl.ds(0, head))
    l_copies = [left_copy(0, 0, pl.ds(head, BS // 2 - head))] + [left_copy(s, *piece(s)) for s in range(1, 4)]

    def exchange(k, q):
        buf = bufs[k * NCH + q]
        copies = []
        for way, (slot, target) in enumerate(((0, up), (2, down))):
            copies.append(pltpu.make_async_remote_copy(
                src_ref=buf.at[1], dst_ref=buf.at[slot], send_sem=x_send.at[k, q, way], recv_sem=x_recv.at[k, q, way],
                device_id={"block": target}, device_id_type=MESH))
        return copies

    moves = [[exchange(k, q) for q in range(NCH)] for k in range(ITERS)]

    pl.semaphore_wait(barrier, entered)
    for copy in [l_head] + l_copies:
        copy.start()

    def send(k, chunks):
        for way, condition in enumerate((has_up, has_down)):
            @pl.when(condition)
            def _():
                for q in chunks:
                    moves[k][q][way].start()

    for q in range(NCH):
        wave_in[q].wait()
        bufs[q][1] = ys[0][:, columns(q)].astype(BF16)
        if q < 0:
            send(0, [q])
    pl.when(jnp.logical_not(even))(functools.partial(send, 0, range(0, NCH)))
    near_start(0)

    hop_in.wait()
    hops = [hop_s[p] for p in range(2)]
    right_in.wait()
    for p in range(2):
        rt_v[p] = right_v[p].astype(F32).T.astype(BF16)

    def blank(slot):
        for buf in bufs:
            buf[slot] = jnp.zeros((BS, CW), BF16)

    pl.when(jnp.logical_not(has_down))(functools.partial(blank, 0))
    pl.when(jnp.logical_not(has_up))(functools.partial(blank, 2))
    diag_in.wait()

    l_head.wait_recv()
    pl.when(even)(functools.partial(send, 0, range(0, NCH)))

    for q in range(NCH):
        m_v[:, columns(q)] = (1.0 + RATE * SHIFT) - RATE * diag_v[:, columns(q)].astype(F32)

    lane = lax.broadcasted_iota(jnp.int32, (1, CW), 1)

    def inner(a, b):
        total = jnp.zeros((8, CW), F32)
        for q in range(NCH):
            total += fold(ys[a][:, columns(q)] * ys[b][:, columns(q)])
        return total

    def placed(pair, total):
        total = jnp.sum(jnp.sum(total, axis=0, keepdims=True), axis=1, keepdims=True)
        return jnp.where(lane == PAIRS.index(pair), total, 0.0)

    every = parts.at[pl.ds(0, nblk - 1)]

    def sums_start(row):
        parts[j] = row
        for dz, dx in others:
            pltpu.make_async_remote_copy(
                src_ref=parts.at[j], dst_ref=parts.at[j], send_sem=sum_sems.at[0], recv_sem=sum_sems.at[1],
                device_id=block_at(dz, dx), device_id_type=MESH).start()

    def arrived(k, q):
        for way, condition in enumerate((has_down, has_up)):
            pl.when(condition)(moves[k][q][way].wait_recv)

    def first_terms(t, chunks, begin=False):
        p, rows = piece(t)
        first = [dot(left_v[p, rows], bufs[q][hops[p]]).astype(BF16) for q in chunks]
        first = jnp.concatenate(first, axis=1)
        more = dot(first, rt_v[p, pl.ds(chunks[0] * CW, len(chunks) * CW)])
        d_v[rows] = more if begin else d_v[rows] + more

    row = jnp.zeros((1, CW), F32)
    last_sums = [jnp.zeros((8, CW), F32)] * ITERS
    for k in range(ITERS):
        last = None
        if k == 0:
            for s in range(NCH - 1):
                arrived(0, s)
                l_copies[s].wait_recv()
                for t in range(s + 1):
                    first_terms(t, range(s + 1) if t == s else [s], t == s and s < 2)

            near_next(0)

            @pl.when(even)
            def _():
                arrived(0, NCH - 1)
                for t in range(NCH - 1):
                    first_terms(t, [NCH - 1])
                l_copies[NCH - 1].wait_recv()
                first_terms(NCH - 1, range(NCH))

            @pl.when(jnp.logical_not(even))
            def _():
                l_copies[NCH - 1].wait_recv()
                first_terms(NCH - 1, range(NCH - 1))
                arrived(0, NCH - 1)
                for t in range(NCH):
                    first_terms(t, [NCH - 1])

        else:
            for q in range(NCH):
                if (k, q) in ((1, 0), (1, NCH - 1)):
                    near_next(1 if q == 0 else 2)
                arrived(k, q)
                first = [dot(left_v[p], bufs[k * NCH + q][hops[p]]).astype(BF16) for p in range(2)]
                first = jnp.concatenate(first, axis=1)
                if q == NCH - 1:
                    last = first
                    break
                more = dot(first, jnp.concatenate([rt_v[p, columns(q)] for p in range(2)], axis=0))
                d_v[...] = more if q == 0 else d_v[...] + more
        for half in range(2):
            wide = pl.ds(half * 2 * CW, 2 * CW)
            if last is not None:
                rights = jnp.concatenate([rt_v[p, columns(NCH - 1), wide] for p in range(2)], axis=0)
                d_v[:, wide] = d_v[:, wide] + dot(last, rights)
            for q in (2 * half, 2 * half + 1):
                y = m_v[:, columns(q)] * ys[k][:, columns(q)] - RATE * d_v[:, columns(q)]
                ys[k + 1][:, columns(q)] = y
                if k < ITERS - 1:
                    bufs[(k + 1) * NCH + q][1] = y.astype(BF16)
                else:
                    for a in range(ITERS):
                        last_sums[a] += fold(ys[a][:, columns(q)] * y)
            if k < ITERS - 1:
                send(k + 1, (2 * half, 2 * half + 1))
        if k < ITERS - 1:
            for pair in PAIRS:
                if pair[1] == k + 1 or (k == 0 and pair == (0, 0)):
                    row = row + placed(pair, inner(*pair))
    for r in range(3, len(reaches)):
        near_next(r)
    for a in range(ITERS):
        row = row + placed((a, ITERS), last_sums[a])
    sums_start(row)
    for copy in [l_head] + l_copies:
        copy.wait_send()
    for way, condition in enumerate((has_up, has_down)):
        @pl.when(condition)
        def _():
            for step in moves:
                for pair in step:
                    pair[way].wait_send()
    pltpu.make_async_copy(every, every, sum_sems.at[1]).wait()
    total = jnp.sum(parts[...], axis=0)
    g = {}
    for i, (a, b) in enumerate(PAIRS):
        g[a, b] = total[0:1, i:i + 1]
    b0 = 1.0 - g[0, 1] / g[0, 0]
    squares = g[1, 1] + b0 * (2.0 * g[0, 1] + b0 * g[0, 0])
    b1 = 1.0 - (g[1, 2] + b0 * (g[1, 1] + g[0, 2] + b0 * g[0, 1])) / squares
    s, t = b0 + b1, b0 * b1
    squares = g[2, 2] + s * (2.0 * g[1, 2] + s * g[1, 1] + 2.0 * t * g[0, 1]) + t * (2.0 * g[0, 2] + t * g[0, 0])
    product = g[2, 3] + s * (g[2, 2] + g[1, 3] + s * g[1, 2] + t * g[1, 1])
    product = product + t * (g[1, 2] + g[0, 3] + s * g[0, 2] + t * g[0, 1])
    b2 = 1.0 - product / squares
    for k, b in enumerate((b0, b1, b2)):
        en_ref[0:1, k:k + 1] = SHIFT + b * (1.0 / RATE)
    one, two, three = s + b2, t + s * b2, t * b2
    for q in range(NCH):
        known = one * ys[2][:, columns(q)] + two * ys[1][:, columns(q)] + three * ys[0][:, columns(q)]
        out_ref[0, :, columns(q)] = ys[3][:, columns(q)] + known
    pltpu.make_async_copy(every, every, sum_sems.at[0]).wait()


def shards(wave, diagonal, left_env, right_env, pair_hop, segs, nblk):
    zg = nblk // XG
    dma = pltpu.SemaphoreType.DMA
    square = pltpu.VMEM((BS, BS), F32)
    vmem = pl.BlockSpec(memory_space=pltpu.VMEM)
    given = [pltpu.with_memory_space_constraint(a, pltpu.HBM) for a in (pair_hop, wave, diagonal, left_env, right_env)]
    return pl.pallas_call(
        functools.partial(kernel, segs, nblk),
        out_shape=(
            jax.ShapeDtypeStruct((1, BS, BS), F32),
            jax.ShapeDtypeStruct((1, ITERS), F32),
        ),
        in_specs=[pl.BlockSpec(memory_space=pl.ANY)] * 5,
        out_specs=(vmem, vmem),
        scratch_shapes=[square] * (ITERS + 1) + [pltpu.VMEM((3, BS, CW), BF16)] * (ITERS * NCH) + [
            pltpu.SMEM((2,), jnp.int32),
            pltpu.VMEM((BS, BS), BF16),
            pltpu.VMEM((2, BS, BS), BF16),
            pltpu.VMEM((2, BS, BS), BF16),
            pltpu.VMEM((2, BS, BS), BF16),
            square, square,
            pltpu.VMEM((nblk, 1, CW), F32),
            dma((NCH + 3,)),
            dma((5,)),
            dma((5,)),
            dma((ITERS, NCH, 2)),
            dma((ITERS, NCH, 2)),
            dma((2,)),
            pltpu.SemaphoreType.REGULAR((zg.bit_length() - 1,)),
        ],
        compiler_params=pltpu.CompilerParams(
            collective_id=0, has_side_effects=True, vmem_limit_bytes=48 * 2 ** 20),
        cost_estimate=pl.CostEstimate(flops=ITERS * 8 * BS ** 3, bytes_accessed=9 * 2 ** 19, transcendentals=0),
    )(*given)


def solution(mesh):
    placed = (
        P("chain", "block", None),
        P("chain", "block", None),
        P("chain", "block", None, None),
        P("chain", "block", None, None),
        P("block"),
    )
    return jax.shard_map(
        functools.partial(shards, segs=mesh.shape["chain"], nblk=mesh.shape["block"]),
        mesh=mesh,
        in_specs=placed,
        out_specs=(P("chain", "block", None), P("chain", None)),
        check_vma=False,
    )
```
